32 devices in a mesh: rep: 2 (over x), row: 4 (over z), col: 4 (over y, core).
Axes of the slice: x: 2, y: 2, z: 4, core: 2. Of those that a mesh axis runs over, the one named last changes fastest.
Arguments:
- coordinates: bfloat16 [8, 32, 3, 128], P('rep')
- resample: int32 [2, 22], P('rep'), may hold values from 0 to 7, as said below
- block_slot: int32 [8], replicated, may hold values from 0 to 7, as said below
- lag_time: int32 [2], P('rep'), may hold values from 1 to 8
- atom_pairs: int32 [2, 4096], replicated, may hold values from 0 to 127, as said below
Outputs:
- instant_cov: bfloat16 [2, 4096, 4096], P('rep', 'row', 'col')
- lagged_cov: bfloat16 [2, 4096, 4096], P('rep', 'row', 'col')
The draws below stay inside these ranges and needn't reach their ends.
Inputs may be any that keep to these rules, and one draw needn't show every extreme that they name: `resample`: the owner of a block is block_slot // 4. In each replicate at most 16 draws have one owner, and some owner has exactly 16; a block may be drawn more than once. `block_slot`: each slot holds exactly one block. `atom_pairs`: the two atoms of a feature differ, and no unordered pair of atoms appears twice.
All inputs are finite; a program needn't handle non-finite values.
Results may differ from the reference program's by a relative error of at most 0.0073.
Values may be sent and summed in bfloat16 or wider, within the bound.
A program may use at most 64 MiB of HBM per device.

```python
import math
import jax
import jax.numpy as jnp
from jax import lax

F = 4096
ATOMS = 128
BLOCK_LEN = 32
DRAWS = 22
LAG_MAX = 8
BLK_DEV = 4
REPLICATES = 2
BLOCKS = 8
CAP = 16


def slot_order(key):
    return jax.random.permutation(jax.random.fold_in(key, 11), BLOCKS).astype(jnp.int32)


def draw_block_slot(key, part):
    return slot_order(key)


def draw_resample(key, part):
    slot_table = slot_order(key)
    inverse = jnp.argsort(slot_table).astype(jnp.int32)
    owner_total = BLOCKS // BLK_DEV
    item_total = owner_total * CAP

    def one_replicate(replicate):
        sub_key = jax.random.fold_in(jax.random.fold_in(key, 23), replicate)
        sub_keys = jax.random.split(sub_key, 4)
        item_place = jnp.argsort(jax.random.permutation(sub_keys[0], item_total)).astype(jnp.int32)
        first_owner = jax.random.randint(sub_keys[1], (), 0, owner_total)
        item_owner = jnp.arange(item_total, dtype=jnp.int32) % owner_total
        item_score = jnp.where(item_owner == first_owner, item_place - item_total, item_place)
        chosen = jnp.argsort(item_score)[:DRAWS].astype(jnp.int32) % owner_total
        chosen = chosen[jax.random.permutation(sub_keys[3], DRAWS)]
        local_slot = jax.random.randint(sub_keys[2], (DRAWS,), 0, BLK_DEV)
        return inverse[chosen * BLK_DEV + local_slot]
    return jax.vmap(one_replicate)(jnp.arange(REPLICATES, dtype=jnp.int32))


def draw_atom_pairs(key, part):
    chosen = jax.random.permutation(jax.random.fold_in(key, 31), ATOMS * (ATOMS // 2 - 1))[:F].astype(jnp.int32)
    first_atoms = chosen % ATOMS
    offsets = chosen // ATOMS + 1
    second_atoms = (first_atoms + offsets) % ATOMS
    return jnp.stack([first_atoms, second_atoms]).astype(jnp.int32)


def draw_coordinates(key, part):
    sub_keys = jax.random.split(jax.random.fold_in(key, 41), 6)
    full_shape = (BLOCKS, BLOCK_LEN, 3, ATOMS)
    center_pos = 2.0 * jax.random.normal(sub_keys[0], (1, 1, 3, ATOMS), jnp.float32)
    block_scale = jnp.exp(jax.random.uniform(sub_keys[1], (BLOCKS, 1, 1, 1), jnp.float32, math.log(0.5), math.log(2.0)))
    frequency = jax.random.uniform(sub_keys[2], (BLOCKS, 1, 3, ATOMS), jnp.float32, 0.1, 0.9)
    phase_shift = jax.random.uniform(sub_keys[3], (BLOCKS, 1, 3, ATOMS), jnp.float32, -math.pi, math.pi)
    amplitude = jax.random.uniform(sub_keys[4], (1, 1, 3, ATOMS), jnp.float32, 0.5, 1.5)
    frame_time = jnp.arange(BLOCK_LEN, dtype=jnp.float32).reshape(1, BLOCK_LEN, 1, 1)
    jitter = 0.4 * jax.random.normal(sub_keys[5], full_shape, jnp.float32)
    values = center_pos + block_scale * (amplitude * jnp.cos(frequency * frame_time + phase_shift) + jitter)
    return values.astype(jnp.bfloat16)


def setup_inputs(seed: int = 0) -> dict:
    key_of = jax.random.split(jax.random.key(seed), 6)
    coordinates = draw_coordinates(jax.random.fold_in(key_of[5], 71), 0)
    resample = draw_resample(jax.random.fold_in(key_of[5], 71), 0)
    block_slot = draw_block_slot(jax.random.fold_in(key_of[5], 71), 0)
    lag_time = jax.random.randint(key_of[3], (REPLICATES,), 1, LAG_MAX + 1).astype(jnp.int32)
    atom_pairs = draw_atom_pairs(jax.random.fold_in(key_of[5], 71), 0)
    return {"coordinates": coordinates, "resample": resample, "block_slot": block_slot, "lag_time": lag_time, "atom_pairs": atom_pairs}


def featurize(blocks_xyz, first_atoms, second_atoms):
    positions = blocks_xyz.astype(jnp.float32)
    difference = positions[..., first_atoms] - positions[..., second_atoms]
    squared = difference[:, :, 0] * difference[:, :, 0] + difference[:, :, 1] * difference[:, :, 1] + difference[:, :, 2] * difference[:, :, 2]
    return jnp.sqrt(squared).astype(jnp.bfloat16)

def centered(features, shift):
    width_total = features.shape[-1]
    doubled = jnp.concatenate([features, features], axis=1)
    shifted = lax.dynamic_slice_in_dim(doubled, shift, BLOCK_LEN, axis=1)
    valid_rows = (jnp.arange(BLOCK_LEN, dtype=jnp.int32) < BLOCK_LEN - shift)[None, :, None]
    pair_count = (2 * DRAWS * (BLOCK_LEN - shift)).astype(jnp.float32)
    earlier = jnp.where(valid_rows, features.astype(jnp.float32), 0.0)
    later = jnp.where(valid_rows, shifted.astype(jnp.float32), 0.0)
    feature_mean = (lax.optimization_barrier(jnp.sum(earlier, axis=(0, 1))) + lax.optimization_barrier(jnp.sum(later, axis=(0, 1)))) / pair_count
    zero_lag = jnp.where(valid_rows, earlier - feature_mean, 0.0).astype(jnp.bfloat16).reshape(-1, width_total)
    lagged = jnp.where(valid_rows, later - feature_mean, 0.0).astype(jnp.bfloat16).reshape(-1, width_total)
    return (zero_lag, lagged, pair_count)

def reference(coordinates, resample, block_slot, lag_time, atom_pairs):

    def one_replicate(inputs):
        drawn_blocks, shift = inputs
        slots = block_slot[drawn_blocks]
        selected = coordinates[slots]
        features = featurize(selected, atom_pairs[0], atom_pairs[1])
        zero_lag, lagged, pair_count = centered(features, shift)
        first_part = zero_lag.astype(jnp.float32)
        second_part = lagged.astype(jnp.float32)
        highest = lax.Precision.HIGHEST
        instant = jnp.dot(first_part.T, first_part, precision=highest) + jnp.dot(second_part.T, second_part, precision=highest)
        crossed = jnp.dot(first_part.T, second_part, precision=highest) + jnp.dot(second_part.T, first_part, precision=highest)
        return ((instant / pair_count).astype(jnp.bfloat16), (crossed / pair_count).astype(jnp.bfloat16))
    instant_cov, lagged_cov = lax.map(one_replicate, (resample, lag_time))
    return (instant_cov, lagged_cov)
```

```python
import functools

import jax
import jax.numpy as jnp
from jax import lax
from jax.experimental import pallas as pl
from jax.experimental.pallas import tpu as pltpu
from jax.sharding import PartitionSpec as P

F = 4096
ATOMS = 128
BLOCK_LEN = 32
DRAWS = 22
TILE = 256
MESH = pl.DeviceIdType.MESH


def slot_lookup(lists, slot_table):
    matches = lists[..., None] == jnp.arange(slot_table.shape[0], dtype=jnp.int32)
    return jnp.sum(jnp.where(matches, slot_table, 0), axis=-1)


def owner_rank(lists, slot_table, blk_count):
    slots = slot_lookup(lists, slot_table)
    owner_ids = slots // blk_count
    local_ids = slots % blk_count
    draw_ids = jnp.arange(lists.shape[-1], dtype=jnp.int32)
    before = (owner_ids[..., :, None] == owner_ids[..., None, :]) & (
        draw_ids[None, :] < draw_ids[:, None]
    )
    ranks = jnp.sum(before.astype(jnp.int32), axis=-1)
    return (owner_ids, local_ids, ranks)


def pack_requests(resample, block_slot, local_data, capacity):
    every_list = lax.all_gather(resample, "rep", axis=0, tiled=True)
    blk_count = local_data.shape[0]
    owners_all, local_all, ranks_all = owner_rank(every_list, block_slot, blk_count)
    myself = lax.axis_index("rep")
    wanted = (owners_all == myself)[:, :, None] & (
        ranks_all[:, :, None] == jnp.arange(capacity, dtype=jnp.int32)
    )
    picked = local_all[:, :, None] == jnp.arange(blk_count, dtype=jnp.int32)
    selector = jnp.einsum(
        "rdc,rdk->rck", wanted.astype(jnp.float32), picked.astype(jnp.float32)
    ).astype(jnp.bfloat16)
    return jnp.einsum(
        "rck,kx->rcx", selector, local_data, preferred_element_type=jnp.float32
    ).astype(jnp.bfloat16)


def unpack_blocks(received, resample, block_slot, blk_count, capacity):
    owner_ids, local_ids, ranks = owner_rank(resample[0], block_slot, blk_count)
    rows_wanted = owner_ids * capacity + ranks
    flat = received.reshape(-1, received.shape[-1])
    return jnp.take(flat, rows_wanted, axis=0)


def drawn_blocks(coordinates, resample, block_slot):
    rep_total = lax.axis_size("rep")
    per_owner = (DRAWS + rep_total - 1) // rep_total
    capacity = max(2, per_owner + per_owner // 2)
    blk_count = coordinates.shape[0]
    outgoing = pack_requests(resample, block_slot, coordinates.reshape(blk_count, -1), capacity)
    received = lax.all_to_all(outgoing, "rep", split_axis=0, concat_axis=0, tiled=True)
    return unpack_blocks(received, resample, block_slot, blk_count, capacity).reshape(
        DRAWS, BLOCK_LEN, 3, ATOMS
    )


def swap_kernel(own_ref, other_ref, send_sem, recv_sem):
    partner = {"rep": 1 - lax.axis_index("rep")}
    barrier = pltpu.get_barrier_semaphore()
    pl.semaphore_signal(barrier, inc=1, device_id=partner, device_id_type=MESH)
    pl.semaphore_wait(barrier, 1)
    copy = pltpu.make_async_remote_copy(
        src_ref=own_ref,
        dst_ref=other_ref,
        send_sem=send_sem,
        recv_sem=recv_sem,
        device_id=partner,
        device_id_type=MESH,
    )
    copy.start()
    copy.wait()


def swap(own):
    return pl.pallas_call(
        swap_kernel,
        out_shape=jax.ShapeDtypeStruct(own.shape, own.dtype),
        in_specs=[pl.BlockSpec(memory_space=pl.ANY)],
        out_specs=pl.BlockSpec(memory_space=pl.ANY),
        scratch_shapes=[pltpu.SemaphoreType.DMA, pltpu.SemaphoreType.DMA],
        compiler_params=pltpu.CompilerParams(collective_id=0, has_side_effects=True),
        name="swap",
    )(own)


def dot(a, b, contract=((1,), (0,))):
    return lax.dot_general(a, b, (contract, ((), ())), preferred_element_type=jnp.float32)


def signed_atoms(pairs_ref, first, width):
    ids = lax.broadcasted_iota(jnp.int32, (ATOMS, width), 0)
    cols = pl.ds(pl.multiple_of(first, TILE), width)
    a = pairs_ref[0:1, cols]
    b = pairs_ref[1:2, cols]
    return jnp.where(ids == a, 1.0, jnp.where(ids == b, -1.0, 0.0))


def distance(parts):
    return jnp.sqrt(parts[0] * parts[0] + parts[1] * parts[1] + parts[2] * parts[2]).astype(
        jnp.bfloat16
    )


def cov_kernel(
    weigh, *refs
):
    lag_ref, draw_ref, slot_ref, pairs_ref, *xyz_refs = refs[:-7]
    inst_ref, lagged_ref, weigh_ref, row_w_ref, col_w_ref, ds_ref, inv_ref = refs[-7:]
    frames = weigh_ref.shape[1]
    width = inst_ref.shape[2]
    lag = lag_ref[0]

    def component(k):
        return jnp.concatenate([ref[k] for ref in xyz_refs], axis=0)

    @pl.when(pl.program_id(0) == 0)
    def _():
        counts = weigh(draw_ref, slot_ref)
        t_row = lax.broadcasted_iota(jnp.int32, (BLOCK_LEN, frames), 0)
        lane = lax.broadcasted_iota(jnp.int32, (BLOCK_LEN, frames), 1)
        t_lane = lane % BLOCK_LEN
        uses_lane = jnp.where(t_lane < BLOCK_LEN - lag, 1.0, 0.0) + jnp.where(
            t_lane >= lag, 1.0, 0.0
        )
        t_col = lax.broadcasted_iota(jnp.int32, (BLOCK_LEN, 128), 0)
        uses_row = jnp.where(t_col < BLOCK_LEN - lag, 1.0, 0.0) + jnp.where(t_col >= lag, 1.0, 0.0)
        row_w = jnp.zeros((BLOCK_LEN, frames), jnp.float32)
        for b, n in enumerate(counts):
            rows = pl.ds(b * BLOCK_LEN, BLOCK_LEN)
            here = lane // BLOCK_LEN == b
            row_w = jnp.where(here, n * uses_lane, row_w)
            weigh_ref[rows, :] = jnp.where(
                here & (t_lane == t_row), n * uses_lane, 0.0
            ).astype(jnp.bfloat16)
            apart = jnp.abs(t_lane - t_row)
            weigh_ref[pl.ds(frames + b * BLOCK_LEN, BLOCK_LEN), :] = jnp.where(
                here & (apart == lag), n, 0.0
            ).astype(jnp.bfloat16)
            col_w_ref[rows, :] = (n * uses_row).astype(jnp.bfloat16)
        row_w_ref[...] = row_w[:16].astype(jnp.bfloat16)
        total = jnp.full((8, 128), (2 * DRAWS * (BLOCK_LEN - lag)).astype(jnp.float32))
        inv_ref[...] = 1.0 / total
        inv = inv_ref[0:1, 0:1]
        first = lax.axis_index("col") * width
        for j in range(width // TILE):
            signed = signed_atoms(pairs_ref, first + j * TILE, TILE).astype(jnp.bfloat16)
            f = distance([dot(component(k), signed) for k in range(3)])
            mean = dot(row_w_ref[...], f)[0:1] * inv
            c = (f.astype(jnp.float32) - mean).astype(jnp.bfloat16)
            ds_ref[:, pl.ds(j * TILE, TILE)] = (dot(weigh_ref[...], c) * inv).astype(jnp.bfloat16)

    inv = inv_ref[0:1, 0:1]
    first = lax.axis_index("row") * (pl.num_programs(0) * TILE) + pl.program_id(0) * TILE
    signed = signed_atoms(pairs_ref, first, TILE).T.astype(jnp.bfloat16)
    f = distance([dot(signed, component(k), ((1,), (1,))) for k in range(3)])
    mean = dot(f, col_w_ref[...]) * inv
    mean = jnp.concatenate([mean] * (frames // 128), axis=1)
    c = (f.astype(jnp.float32) - mean).astype(jnp.bfloat16)
    inst_ref[0] = dot(c, ds_ref[pl.ds(0, frames), :]).astype(jnp.bfloat16)
    lagged_ref[0] = dot(c, ds_ref[pl.ds(frames, frames), :]).astype(jnp.bfloat16)


def covariances(xyz, weigh, lag_time, resample, block_slot, atom_pairs):
    frames = sum(x.shape[1] for x in xyz)
    height = F // lax.axis_size("row")
    width = F // lax.axis_size("col")
    smem = pl.BlockSpec(memory_space=pltpu.SMEM)
    vmem = pl.BlockSpec(memory_space=pltpu.VMEM)
    out = jax.ShapeDtypeStruct((1, height, width), jnp.bfloat16)
    out_spec = pl.BlockSpec((1, TILE, width), lambda i: (0, i, 0))
    return pl.pallas_call(
        functools.partial(cov_kernel, weigh),
        grid=(height // TILE,),
        out_shape=(out, out),
        in_specs=[smem, smem, smem, vmem] + [vmem] * len(xyz),
        out_specs=(out_spec, out_spec),
        scratch_shapes=[
            pltpu.VMEM((2 * frames, frames), jnp.bfloat16),
            pltpu.VMEM((16, frames), jnp.bfloat16),
            pltpu.VMEM((frames, 128), jnp.bfloat16),
            pltpu.VMEM((2 * frames, width), jnp.bfloat16),
            pltpu.VMEM((8, 128), jnp.float32),
        ],
        compiler_params=pltpu.CompilerParams(vmem_limit_bytes=48 * 1024 * 1024),
        name="covariances",
    )(lag_time, resample.reshape(-1), block_slot, atom_pairs, *xyz)


def by_component(blocks):
    return blocks.transpose(2, 0, 1, 3).reshape(3, -1, ATOMS)


def shards(coordinates, resample, block_slot, lag_time, atom_pairs):
    rep_total = lax.axis_size("rep")
    blk_count = coordinates.shape[0]
    if rep_total == 2 and 2 * blk_count <= DRAWS:
        own = by_component(coordinates)
        xyz = [own, swap(own)]

        def weigh(draw_ref, slot_ref):
            mine = lax.axis_index("rep") * blk_count
            slots = [slot_ref[draw_ref[d]] for d in range(DRAWS)]
            first = [mine, blk_count - mine]
            return [
                sum(jnp.where(s == first[half] + b, 1.0, 0.0) for s in slots)
                for half in range(2)
                for b in range(blk_count)
            ]
    else:
        blocks = drawn_blocks(coordinates, resample, block_slot)
        spare = -DRAWS % (128 // BLOCK_LEN)
        blocks = jnp.pad(blocks, ((0, spare), (0, 0), (0, 0), (0, 0)))
        xyz = [by_component(blocks)]

        def weigh(draw_ref, slot_ref):
            return [1.0] * DRAWS + [0.0] * spare
    return covariances(xyz, weigh, lag_time, resample, block_slot, atom_pairs)


def solution(mesh):
    return jax.shard_map(
        shards,
        mesh=mesh,
        in_specs=(P("rep", None, None, None), P("rep", None), P(), P("rep"), P()),
        out_specs=(P("rep", "row", "col"), P("rep", "row", "col")),
        check_vma=False,
    )
```

```python
import functools

import jax
import jax.numpy as jnp
from jax import lax
from jax.experimental import pallas as pl
from jax.experimental.pallas import tpu as pltpu
from jax.sharding import PartitionSpec as P

F = 4096
ATOMS = 128
BLOCK_LEN = 32
DRAWS = 22
TILE = 256
TINY = 1.2e-38
VMEM_BYTES = 60 * 1024 * 1024
MESH = pl.DeviceIdType.MESH


def slot_lookup(lists, slot_table):
    matches = lists[..., None] == jnp.arange(slot_table.shape[0], dtype=jnp.int32)
    return jnp.sum(jnp.where(matches, slot_table, 0), axis=-1)


def owner_rank(lists, slot_table, blk_count):
    slots = slot_lookup(lists, slot_table)
    owner_ids = slots // blk_count
    local_ids = slots % blk_count
    draw_ids = jnp.arange(lists.shape[-1], dtype=jnp.int32)
    before = (owner_ids[..., :, None] == owner_ids[..., None, :]) & (
        draw_ids[None, :] < draw_ids[:, None]
    )
    ranks = jnp.sum(before.astype(jnp.int32), axis=-1)
    return (owner_ids, local_ids, ranks)


def pack_requests(resample, block_slot, local_data, capacity):
    every_list = lax.all_gather(resample, "rep", axis=0, tiled=True)
    blk_count = local_data.shape[0]
    owners_all, local_all, ranks_all = owner_rank(every_list, block_slot, blk_count)
    myself = lax.axis_index("rep")
    wanted = (owners_all == myself)[:, :, None] & (
        ranks_all[:, :, None] == jnp.arange(capacity, dtype=jnp.int32)
    )
    picked = local_all[:, :, None] == jnp.arange(blk_count, dtype=jnp.int32)
    selector = jnp.einsum(
        "rdc,rdk->rck", wanted.astype(jnp.float32), picked.astype(jnp.float32)
    ).astype(jnp.bfloat16)
    return jnp.einsum(
        "rck,kx->rcx", selector, local_data, preferred_element_type=jnp.float32
    ).astype(jnp.bfloat16)


def unpack_blocks(received, resample, block_slot, blk_count, capacity):
    owner_ids, local_ids, ranks = owner_rank(resample[0], block_slot, blk_count)
    rows_wanted = owner_ids * capacity + ranks
    flat = received.reshape(-1, received.shape[-1])
    return jnp.take(flat, rows_wanted, axis=0)


def drawn_blocks(coordinates, resample, block_slot):
    rep_total = lax.axis_size("rep")
    per_owner = (DRAWS + rep_total - 1) // rep_total
    capacity = max(2, per_owner + per_owner // 2)
    blk_count = coordinates.shape[0]
    outgoing = pack_requests(resample, block_slot, coordinates.reshape(blk_count, -1), capacity)
    received = lax.all_to_all(outgoing, "rep", split_axis=0, concat_axis=0, tiled=True)
    return unpack_blocks(received, resample, block_slot, blk_count, capacity).reshape(
        DRAWS, BLOCK_LEN, 3, ATOMS
    )


def dot(a, b):
    return jnp.dot(a, b, preferred_element_type=jnp.float32)


def signed_atoms(pairs_ref, first):
    ids = lax.broadcasted_iota(jnp.int32, (ATOMS, TILE), 0)
    cols = pl.ds(pl.multiple_of(first, TILE), TILE)
    a = pairs_ref[0:1, cols]
    b = pairs_ref[1:2, cols]
    return jnp.where(ids == a, 1.0, jnp.where(ids == b, -1.0, 0.0)).astype(jnp.bfloat16)


def features(blocks_ref, signed):
    squared = 0.0
    for k in range(3):
        difference = dot(blocks_ref[:, k].reshape(-1, ATOMS), signed)
        squared = squared + difference * difference
    return (squared * lax.rsqrt(jnp.maximum(squared, TINY))).astype(jnp.bfloat16)


def near_kernel(partnered, weigh, *refs):
    outs, scratch = refs[5:-11], refs[-11:]
    lag_ref = refs[4]
    blocks_ref, draw_ref, slot_ref, pairs_ref = scratch[:4]
    built = col_ref, row_ref, weigh_ref, inv_ref = scratch[4:8]
    sems, send_sem, recv_sem = scratch[8:]
    frames = weigh_ref.shape[1]

    if partnered:
        partner = {"rep": 1 - lax.axis_index("rep")}
        barrier = pltpu.get_barrier_semaphore()
        pl.semaphore_signal(barrier, inc=1, device_id=partner, device_id_type=MESH)
    fetches = [
        pltpu.make_async_copy(src, dst, sems.at[i])
        for i, (src, dst) in enumerate(zip(refs[:4], scratch[:4]))
    ]
    for fetch in fetches:
        fetch.start()
    if partnered:
        pl.semaphore_wait(barrier, 1)
        copy = pltpu.make_async_remote_copy(
            src_ref=refs[0],
            dst_ref=outs[4],
            send_sem=send_sem,
            recv_sem=recv_sem,
            device_id=partner,
            device_id_type=MESH,
        )
        copy.start()
    for fetch in fetches:
        fetch.wait()

    stores = [
        pltpu.make_async_copy(src, dst, sems.at[4 + i])
        for i, (src, dst) in enumerate(zip(built, outs[:4]))
    ]
    for i, axis in enumerate(("col", "row")):
        side_ref = built[i]
        width = side_ref.shape[1]
        for j in range(width // TILE):
            cols = pl.ds(j * TILE, TILE)
            signed = signed_atoms(pairs_ref, lax.axis_index(axis) * width + j * TILE)
            side_ref[:ATOMS, cols] = signed
            side_ref[ATOMS:, cols] = features(blocks_ref, signed)
        stores[i].start()

    lag = lag_ref[0]
    counts = weigh(draw_ref, slot_ref)
    t_row = lax.broadcasted_iota(jnp.int32, (BLOCK_LEN, frames), 0)
    lane = lax.broadcasted_iota(jnp.int32, (BLOCK_LEN, frames), 1)
    t_lane = lane % BLOCK_LEN
    uses = jnp.where(t_lane < BLOCK_LEN - lag, 1.0, 0.0) + jnp.where(t_lane >= lag, 1.0, 0.0)
    same = jnp.where(t_lane == t_row, uses, 0.0)
    apart = jnp.where(jnp.abs(t_lane - t_row) == lag, 1.0, 0.0)
    mean_w = jnp.zeros((BLOCK_LEN, frames), jnp.float32)
    for b, n in enumerate(counts):
        share = jnp.where(lane // BLOCK_LEN == b, n, 0.0)
        mean_w = mean_w + share * uses
        weigh_ref[pl.ds(b * BLOCK_LEN, BLOCK_LEN), :] = (share * same).astype(jnp.bfloat16)
        weigh_ref[pl.ds(frames + b * BLOCK_LEN, BLOCK_LEN), :] = (share * apart).astype(
            jnp.bfloat16
        )
    weigh_ref[pl.ds(2 * frames, 16), :] = mean_w[:16].astype(jnp.bfloat16)
    inv_ref[...] = 1.0 / jnp.full((8, 128), (2 * DRAWS * (BLOCK_LEN - lag)).astype(jnp.float32))
    for store in stores[2:]:
        store.start()
    for store in stores:
        store.wait()
    if partnered:
        copy.wait()


def near_side(blocks, partnered, weigh, lag_time, resample, block_slot, atom_pairs):
    held = blocks.shape[0] * BLOCK_LEN
    frames = held * (2 if partnered else 1)
    built = [
        ((ATOMS + held, F // lax.axis_size("col")), jnp.bfloat16),
        ((ATOMS + held, F // lax.axis_size("row")), jnp.bfloat16),
        ((2 * frames + 16, frames), jnp.bfloat16),
        ((8, 128), jnp.float32),
    ]
    outs = [jax.ShapeDtypeStruct(*shape) for shape in built]
    if partnered:
        outs.append(jax.ShapeDtypeStruct(blocks.shape, blocks.dtype))
    return pl.pallas_call(
        functools.partial(near_kernel, partnered, weigh),
        out_shape=outs,
        in_specs=[pl.BlockSpec(memory_space=pltpu.HBM)] * 4
        + [pl.BlockSpec(memory_space=pltpu.SMEM)],
        out_specs=[pl.BlockSpec(memory_space=pltpu.HBM)] * len(outs),
        scratch_shapes=[
            pltpu.VMEM(blocks.shape, blocks.dtype),
            pltpu.SMEM(resample.shape, jnp.int32),
            pltpu.SMEM(block_slot.shape, jnp.int32),
            pltpu.VMEM(atom_pairs.shape, jnp.int32),
            *[pltpu.VMEM(*shape) for shape in built],
            pltpu.SemaphoreType.DMA((8,)),
            pltpu.SemaphoreType.DMA,
            pltpu.SemaphoreType.DMA,
        ],
        compiler_params=pltpu.CompilerParams(
            vmem_limit_bytes=VMEM_BYTES,
            **(dict(collective_id=0, has_side_effects=True) if partnered else {}),
        ),
        name="near_side",
    )(blocks, resample, block_slot, atom_pairs, lag_time)


def cov_kernel(inputs, *refs):
    inst_ref, lagged_ref = refs[inputs : inputs + 2]
    held_refs, ds_ref, sems = refs[inputs + 2 : -2], refs[-2], refs[-1]
    col_ref, row_ref, weigh_ref, inv_ref, *far_refs = held_refs
    frames = weigh_ref.shape[1]

    def centred(side_ref, first):
        cols = pl.ds(pl.multiple_of(first, TILE), TILE)
        parts = [side_ref[ATOMS:, cols]]
        parts += [features(far_ref, side_ref[:ATOMS, cols]) for far_ref in far_refs]
        f = jnp.concatenate(parts, axis=0)
        mean = dot(weigh_ref[pl.ds(2 * frames, 16), :], f)[0:1] * inv_ref[0:1, 0:1]
        return f.astype(jnp.float32) - mean

    @pl.when(pl.program_id(0) == 0)
    def _():
        fetches = [
            pltpu.make_async_copy(refs[i], held_refs[i], sems.at[i]) for i in range(inputs)
        ]
        order = [i for i in range(inputs) if i != 1]
        for i in order + [1]:
            fetches[i].start()
        for i in order:
            fetches[i].wait()
        for j in range(ds_ref.shape[1] // TILE):
            c = centred(col_ref, j * TILE).astype(jnp.bfloat16)
            ds_ref[:, pl.ds(j * TILE, TILE)] = (
                dot(weigh_ref[pl.ds(0, 2 * frames), :], c) * inv_ref[0:1, 0:1]
            ).astype(jnp.bfloat16)
        fetches[1].wait()

    c = centred(row_ref, pl.program_id(0) * TILE).T.astype(jnp.bfloat16)
    inst_ref[0] = dot(c, ds_ref[pl.ds(0, frames), :]).astype(jnp.bfloat16)
    lagged_ref[0] = dot(c, ds_ref[pl.ds(frames, frames), :]).astype(jnp.bfloat16)


def covariances(sides):
    frames = sides[2].shape[1]
    height = F // lax.axis_size("row")
    width = F // lax.axis_size("col")
    out = jax.ShapeDtypeStruct((1, height, width), jnp.bfloat16)
    out_spec = pl.BlockSpec((1, TILE, width), lambda i: (0, i, 0))
    return pl.pallas_call(
        functools.partial(cov_kernel, len(sides)),
        grid=(height // TILE,),
        out_shape=(out, out),
        in_specs=[pl.BlockSpec(memory_space=pltpu.HBM)] * len(sides),
        out_specs=(out_spec, out_spec),
        scratch_shapes=[
            *[pltpu.VMEM(side.shape, side.dtype) for side in sides],
            pltpu.VMEM((2 * frames, width), jnp.bfloat16),
            pltpu.SemaphoreType.DMA((len(sides),)),
        ],
        compiler_params=pltpu.CompilerParams(vmem_limit_bytes=VMEM_BYTES),
        name="covariances",
    )(*sides)


def shards(coordinates, resample, block_slot, lag_time, atom_pairs):
    blk_count = coordinates.shape[0]
    partnered = lax.axis_size("rep") == 2 and 2 * blk_count <= DRAWS
    if partnered:
        blocks = coordinates

        def weigh(draw_ref, slot_ref):
            mine = lax.axis_index("rep") * blk_count
            slots = [slot_ref[draw_ref[0, d]] for d in range(DRAWS)]
            return [
                sum(jnp.where(s == first + b, 1.0, 0.0) for s in slots)
                for first in (mine, blk_count - mine)
                for b in range(blk_count)
            ]
    else:
        spare = -DRAWS % (128 // BLOCK_LEN)
        blocks = drawn_blocks(coordinates, resample, block_slot)
        blocks = jnp.pad(blocks, ((0, spare), (0, 0), (0, 0), (0, 0)))

        def weigh(draw_ref, slot_ref):
            return [1.0] * DRAWS + [0.0] * spare
    sides = near_side(
        blocks.transpose(0, 2, 1, 3), partnered, weigh, lag_time, resample, block_slot, atom_pairs
    )
    return covariances(sides)


def solution(mesh):
    return jax.shard_map(
        shards,
        mesh=mesh,
        in_specs=(P("rep", None, None, None), P("rep", None), P(), P("rep"), P()),
        out_specs=(P("rep", "row", "col"), P("rep", "row", "col")),
        check_vma=False,
    )
```

```python
import functools

import jax
import jax.numpy as jnp
from jax import lax
from jax.experimental import pallas as pl
from jax.experimental.pallas import tpu as pltpu
from jax.sharding import PartitionSpec as P

F = 4096
ATOMS = 128
BLOCK_LEN = 32
DRAWS = 22
TILE = 256
TINY = 1.2e-38
VMEM_BYTES = 60 * 1024 * 1024
MESH = pl.DeviceIdType.MESH


def slot_lookup(lists, slot_table):
    matches = lists[..., None] == jnp.arange(slot_table.shape[0], dtype=jnp.int32)
    return jnp.sum(jnp.where(matches, slot_table, 0), axis=-1)


def owner_rank(lists, slot_table, blk_count):
    slots = slot_lookup(lists, slot_table)
    owner_ids = slots // blk_count
    local_ids = slots % blk_count
    draw_ids = jnp.arange(lists.shape[-1], dtype=jnp.int32)
    before = (owner_ids[..., :, None] == owner_ids[..., None, :]) & (
        draw_ids[None, :] < draw_ids[:, None]
    )
    ranks = jnp.sum(before.astype(jnp.int32), axis=-1)
    return (owner_ids, local_ids, ranks)


def pack_requests(resample, block_slot, local_data, capacity):
    every_list = lax.all_gather(resample, "rep", axis=0, tiled=True)
    blk_count = local_data.shape[0]
    owners_all, local_all, ranks_all = owner_rank(every_list, block_slot, blk_count)
    myself = lax.axis_index("rep")
    wanted = (owners_all == myself)[:, :, None] & (
        ranks_all[:, :, None] == jnp.arange(capacity, dtype=jnp.int32)
    )
    picked = local_all[:, :, None] == jnp.arange(blk_count, dtype=jnp.int32)
    selector = jnp.einsum(
        "rdc,rdk->rck", wanted.astype(jnp.float32), picked.astype(jnp.float32)
    ).astype(jnp.bfloat16)
    return jnp.einsum(
        "rck,kx->rcx", selector, local_data, preferred_element_type=jnp.float32
    ).astype(jnp.bfloat16)


def unpack_blocks(received, resample, block_slot, blk_count, capacity):
    owner_ids, local_ids, ranks = owner_rank(resample[0], block_slot, blk_count)
    rows_wanted = owner_ids * capacity + ranks
    flat = received.reshape(-1, received.shape[-1])
    return jnp.take(flat, rows_wanted, axis=0)


def drawn_blocks(coordinates, resample, block_slot):
    rep_total = lax.axis_size("rep")
    per_owner = (DRAWS + rep_total - 1) // rep_total
    capacity = max(2, per_owner + per_owner // 2)
    blk_count = coordinates.shape[0]
    outgoing = pack_requests(resample, block_slot, coordinates.reshape(blk_count, -1), capacity)
    received = lax.all_to_all(outgoing, "rep", split_axis=0, concat_axis=0, tiled=True)
    return unpack_blocks(received, resample, block_slot, blk_count, capacity).reshape(
        DRAWS, BLOCK_LEN, 3, ATOMS
    )


def dot(a, b):
    return jnp.dot(a, b, preferred_element_type=jnp.float32)


def signed_atoms(pairs_ref, first):
    ids = lax.broadcasted_iota(jnp.int32, (ATOMS, TILE), 0)
    cols = pl.ds(pl.multiple_of(first, TILE), TILE)
    a = pairs_ref[0:1, cols]
    b = pairs_ref[1:2, cols]
    return jnp.where(ids == a, 1.0, jnp.where(ids == b, -1.0, 0.0)).astype(jnp.bfloat16)


def features(blocks_ref, signed):
    squared = 0.0
    for k in range(3):
        difference = dot(blocks_ref[:, k].reshape(-1, ATOMS), signed)
        squared = squared + difference * difference
    return (squared * lax.rsqrt(jnp.maximum(squared, TINY))).astype(jnp.bfloat16)


def near_kernel(partnered, weigh, *refs):
    outs, scratch = refs[5:-11], refs[-11:]
    lag_ref = refs[4]
    blocks_ref, draw_ref, slot_ref, pairs_ref = scratch[:4]
    built = col_ref, row_ref, weigh_ref, inv_ref = scratch[4:8]
    sems, send_sem, recv_sem = scratch[8:]
    frames = weigh_ref.shape[1]

    if partnered:
        partner = {"rep": 1 - lax.axis_index("rep")}
        barrier = pltpu.get_barrier_semaphore()
        pl.semaphore_signal(barrier, inc=1, device_id=partner, device_id_type=MESH)
    fetches = [
        pltpu.make_async_copy(src, dst, sems.at[i])
        for i, (src, dst) in enumerate(zip(refs[:4], scratch[:4]))
    ]
    for fetch in fetches:
        fetch.start()
    if partnered:
        pl.semaphore_wait(barrier, 1)
        copy = pltpu.make_async_remote_copy(
            src_ref=refs[0],
            dst_ref=outs[4],
            send_sem=send_sem,
            recv_sem=recv_sem,
            device_id=partner,
            device_id_type=MESH,
        )
        copy.start()
    for fetch in fetches:
        fetch.wait()

    stores = [
        pltpu.make_async_copy(src, dst, sems.at[4 + i])
        for i, (src, dst) in enumerate(zip(built, outs[:4]))
    ]
    for i, axis in enumerate(("col", "row")):
        side_ref = built[i]
        width = side_ref.shape[1]
        for j in range(width // TILE):
            cols = pl.ds(j * TILE, TILE)
            signed = signed_atoms(pairs_ref, lax.axis_index(axis) * width + j * TILE)
            side_ref[:ATOMS, cols] = signed
            side_ref[ATOMS:, cols] = features(blocks_ref, signed)
        stores[i].start()

    lag = lag_ref[0]
    counts = weigh(draw_ref, slot_ref)
    t_row = lax.broadcasted_iota(jnp.int32, (BLOCK_LEN, frames), 0)
    lane = lax.broadcasted_iota(jnp.int32, (BLOCK_LEN, frames), 1)
    t_lane = lane % BLOCK_LEN
    uses = jnp.where(t_lane < BLOCK_LEN - lag, 1.0, 0.0) + jnp.where(t_lane >= lag, 1.0, 0.0)
    same = jnp.where(t_lane == t_row, uses, 0.0)
    apart = jnp.where(jnp.abs(t_lane - t_row) == lag, 1.0, 0.0)
    mean_w = jnp.zeros((BLOCK_LEN, frames), jnp.float32)
    for b, n in enumerate(counts):
        share = jnp.where(lane // BLOCK_LEN == b, n, 0.0)
        mean_w = mean_w + share * uses
        weigh_ref[pl.ds(b * BLOCK_LEN, BLOCK_LEN), :] = (share * same).astype(jnp.bfloat16)
        weigh_ref[pl.ds(frames + b * BLOCK_LEN, BLOCK_LEN), :] = (share * apart).astype(
            jnp.bfloat16
        )
    weigh_ref[pl.ds(2 * frames, 16), :] = mean_w[:16].astype(jnp.bfloat16)
    inv_ref[...] = 1.0 / jnp.full((8, 128), (2 * DRAWS * (BLOCK_LEN - lag)).astype(jnp.float32))
    for store in stores[2:]:
        store.start()
    for store in stores:
        store.wait()
    if partnered:
        copy.wait()


def near_side(blocks, partnered, weigh, lag_time, resample, block_slot, atom_pairs):
    held = blocks.shape[0] * BLOCK_LEN
    frames = held * (2 if partnered else 1)
    built = [
        ((ATOMS + held, F // lax.axis_size("col")), jnp.bfloat16),
        ((ATOMS + held, F // lax.axis_size("row")), jnp.bfloat16),
        ((2 * frames + 16, frames), jnp.bfloat16),
        ((8, 128), jnp.float32),
    ]
    outs = [jax.ShapeDtypeStruct(*shape) for shape in built]
    if partnered:
        outs.append(jax.ShapeDtypeStruct(blocks.shape, blocks.dtype))
    return pl.pallas_call(
        functools.partial(near_kernel, partnered, weigh),
        out_shape=outs,
        in_specs=[pl.BlockSpec(memory_space=pltpu.HBM)] * 4
        + [pl.BlockSpec(memory_space=pltpu.SMEM)],
        out_specs=[pl.BlockSpec(memory_space=pltpu.HBM)] * len(outs),
        scratch_shapes=[
            pltpu.VMEM(blocks.shape, blocks.dtype),
            pltpu.SMEM(resample.shape, jnp.int32),
            pltpu.SMEM(block_slot.shape, jnp.int32),
            pltpu.VMEM(atom_pairs.shape, jnp.int32),
            *[pltpu.VMEM(*shape) for shape in built],
            pltpu.SemaphoreType.DMA((8,)),
            pltpu.SemaphoreType.DMA,
            pltpu.SemaphoreType.DMA,
        ],
        compiler_params=pltpu.CompilerParams(
            vmem_limit_bytes=VMEM_BYTES,
            **(dict(collective_id=0, has_side_effects=True) if partnered else {}),
        ),
        name="near_side",
    )(blocks, resample, block_slot, atom_pairs, lag_time)


def cov_kernel(inputs, *refs):
    inst_ref, lagged_ref = refs[inputs : inputs + 2]
    held_refs = refs[inputs + 2 : -4]
    c_ref, turned_ref, ds_ref, sems = refs[-4:]
    col_ref, row_ref, weigh_ref, inv_ref, *far_refs = held_refs
    frames = weigh_ref.shape[1]
    inv = lambda: inv_ref[0:1, 0:1]

    @pl.when(pl.program_id(0) == 0)
    def _():
        fetches = [
            pltpu.make_async_copy(
                src, dst.at[pl.ds(0, src.shape[0])] if i < 2 else dst, sems.at[i]
            )
            for i, (src, dst) in enumerate(zip(refs[:inputs], held_refs))
        ]
        for fetch in fetches:
            fetch.start()
        for fetch in fetches:
            fetch.wait()
        for side_ref in (col_ref, row_ref):
            for j in range(side_ref.shape[1] // TILE):
                cols = pl.ds(j * TILE, TILE)
                at = ATOMS + frames - len(far_refs) * (frames // 2)
                for far_ref in far_refs:
                    side_ref[at:, cols] = features(far_ref, side_ref[:ATOMS, cols])
        mean_w = weigh_ref[pl.ds(2 * frames, 16), :]
        means = [
            dot(mean_w, side_ref[ATOMS:, :])[0:1] * inv() for side_ref in (col_ref, row_ref)
        ]
        for j in range(ds_ref.shape[0]):
            cols = pl.ds(j * TILE, TILE)
            f = col_ref[ATOMS:, cols].astype(jnp.float32)
            c_ref[:, cols] = (f - means[0][:, j * TILE : (j + 1) * TILE]).astype(jnp.bfloat16)
        for j in range(turned_ref.shape[0] // TILE):
            cols = pl.ds(j * TILE, TILE)
            f = row_ref[ATOMS:, cols].astype(jnp.float32)
            c = (f - means[1][:, j * TILE : (j + 1) * TILE]).astype(jnp.bfloat16)
            turned_ref[cols, :] = c.T
        for j in range(ds_ref.shape[0]):
            ds_ref[j] = (
                dot(weigh_ref[pl.ds(0, 2 * frames), :], c_ref[:, pl.ds(j * TILE, TILE)]) * inv()
            ).astype(jnp.bfloat16)

    j = pl.program_id(0)
    c = turned_ref[...]
    inst_ref[0] = dot(c, ds_ref[j, pl.ds(0, frames), :]).astype(jnp.bfloat16)
    lagged_ref[0] = dot(c, ds_ref[j, pl.ds(frames, frames), :]).astype(jnp.bfloat16)


def covariances(sides):
    frames = sides[2].shape[1]
    height = F // lax.axis_size("row")
    width = F // lax.axis_size("col")
    out = jax.ShapeDtypeStruct((1, height, width), jnp.bfloat16)
    out_spec = pl.BlockSpec((1, height, TILE), lambda j: (0, 0, j))
    return pl.pallas_call(
        functools.partial(cov_kernel, len(sides)),
        grid=(width // TILE,),
        out_shape=(out, out),
        in_specs=[pl.BlockSpec(memory_space=pltpu.HBM)] * len(sides),
        out_specs=(out_spec, out_spec),
        scratch_shapes=[
            pltpu.VMEM((ATOMS + frames, width), jnp.bfloat16),
            pltpu.VMEM((ATOMS + frames, height), jnp.bfloat16),
            *[pltpu.VMEM(side.shape, side.dtype) for side in sides[2:]],
            pltpu.VMEM((frames, width), jnp.bfloat16),
            pltpu.VMEM((height, frames), jnp.bfloat16),
            pltpu.VMEM((width // TILE, 2 * frames, TILE), jnp.bfloat16),
            pltpu.SemaphoreType.DMA((len(sides),)),
        ],
        compiler_params=pltpu.CompilerParams(vmem_limit_bytes=VMEM_BYTES),
        name="covariances",
    )(*sides)


def shards(coordinates, resample, block_slot, lag_time, atom_pairs):
    blk_count = coordinates.shape[0]
    partnered = lax.axis_size("rep") == 2 and 2 * blk_count <= DRAWS
    if partnered:
        blocks = coordinates

        def weigh(draw_ref, slot_ref):
            mine = lax.axis_index("rep") * blk_count
            slots = [slot_ref[draw_ref[0, d]] for d in range(DRAWS)]
            return [
                sum(jnp.where(s == first + b, 1.0, 0.0) for s in slots)
                for first in (mine, blk_count - mine)
                for b in range(blk_count)
            ]
    else:
        spare = -DRAWS % (128 // BLOCK_LEN)
        blocks = drawn_blocks(coordinates, resample, block_slot)
        blocks = jnp.pad(blocks, ((0, spare), (0, 0), (0, 0), (0, 0)))

        def weigh(draw_ref, slot_ref):
            return [1.0] * DRAWS + [0.0] * spare
    sides = near_side(
        blocks.transpose(0, 2, 1, 3), partnered, weigh, lag_time, resample, block_slot, atom_pairs
    )
    return covariances(sides)


def solution(mesh):
    return jax.shard_map(
        shards,
        mesh=mesh,
        in_specs=(P("rep", None, None, None), P("rep", None), P(), P("rep"), P()),
        out_specs=(P("rep", "row", "col"), P("rep", "row", "col")),
        check_vma=False,
    )
```

```python
import functools

import jax
import jax.numpy as jnp
from jax import lax
from jax.experimental import pallas as pl
from jax.experimental.pallas import tpu as pltpu
from jax.sharding import PartitionSpec as P

F = 4096
ATOMS = 128
BLOCK_LEN = 32
DRAWS = 22
TILE = 256
TINY = 1.2e-38
VMEM_BYTES = 60 * 1024 * 1024
MESH = pl.DeviceIdType.MESH


def slot_lookup(lists, slot_table):
    matches = lists[..., None] == jnp.arange(slot_table.shape[0], dtype=jnp.int32)
    return jnp.sum(jnp.where(matches, slot_table, 0), axis=-1)


def owner_rank(lists, slot_table, blk_count):
    slots = slot_lookup(lists, slot_table)
    owner_ids = slots // blk_count
    local_ids = slots % blk_count
    draw_ids = jnp.arange(lists.shape[-1], dtype=jnp.int32)
    before = (owner_ids[..., :, None] == owner_ids[..., None, :]) & (
        draw_ids[None, :] < draw_ids[:, None]
    )
    ranks = jnp.sum(before.astype(jnp.int32), axis=-1)
    return (owner_ids, local_ids, ranks)


def pack_requests(resample, block_slot, local_data, capacity):
    every_list = lax.all_gather(resample, "rep", axis=0, tiled=True)
    blk_count = local_data.shape[0]
    owners_all, local_all, ranks_all = owner_rank(every_list, block_slot, blk_count)
    myself = lax.axis_index("rep")
    wanted = (owners_all == myself)[:, :, None] & (
        ranks_all[:, :, None] == jnp.arange(capacity, dtype=jnp.int32)
    )
    picked = local_all[:, :, None] == jnp.arange(blk_count, dtype=jnp.int32)
    selector = jnp.einsum(
        "rdc,rdk->rck", wanted.astype(jnp.float32), picked.astype(jnp.float32)
    ).astype(jnp.bfloat16)
    return jnp.einsum(
        "rck,kx->rcx", selector, local_data, preferred_element_type=jnp.float32
    ).astype(jnp.bfloat16)


def unpack_blocks(received, resample, block_slot, blk_count, capacity):
    owner_ids, local_ids, ranks = owner_rank(resample[0], block_slot, blk_count)
    rows_wanted = owner_ids * capacity + ranks
    flat = received.reshape(-1, received.shape[-1])
    return jnp.take(flat, rows_wanted, axis=0)


def drawn_blocks(coordinates, resample, block_slot):
    rep_total = lax.axis_size("rep")
    per_owner = (DRAWS + rep_total - 1) // rep_total
    capacity = max(2, per_owner + per_owner // 2)
    blk_count = coordinates.shape[0]
    outgoing = pack_requests(resample, block_slot, coordinates.reshape(blk_count, -1), capacity)
    received = lax.all_to_all(outgoing, "rep", split_axis=0, concat_axis=0, tiled=True)
    return unpack_blocks(received, resample, block_slot, blk_count, capacity).reshape(
        DRAWS, BLOCK_LEN, 3, ATOMS
    )


def dot(a, b):
    return jnp.dot(a, b, preferred_element_type=jnp.float32)


def signed_atoms(pairs_ref, first):
    ids = lax.broadcasted_iota(jnp.int32, (ATOMS, TILE), 0)
    cols = pl.ds(pl.multiple_of(first, TILE), TILE)
    a = pairs_ref[0:1, cols]
    b = pairs_ref[1:2, cols]
    return jnp.where(ids == a, 1.0, jnp.where(ids == b, -1.0, 0.0)).astype(jnp.bfloat16)


def features(blocks_ref, signed):
    squared = 0.0
    for k in range(3):
        difference = dot(blocks_ref[:, k].reshape(-1, ATOMS), signed)
        squared = squared + difference * difference
    return (squared * lax.rsqrt(jnp.maximum(squared, TINY))).astype(jnp.bfloat16)


def near_kernel(partnered, weigh, *refs):
    outs, scratch = refs[5:-11], refs[-11:]
    lag_ref = refs[4]
    blocks_ref, draw_ref, slot_ref, pairs_ref = scratch[:4]
    built = col_ref, row_ref, weigh_ref, inv_ref = scratch[4:8]
    sems, send_sem, recv_sem = scratch[8:]
    frames = weigh_ref.shape[1]

    if partnered:
        partner = {"rep": 1 - lax.axis_index("rep")}
        barrier = pltpu.get_barrier_semaphore()
        me = lax.axis_index("col")
        part = me % 2
        twin = {"col": me + 1 - 2 * part}
        for other in (partner, twin):
            pl.semaphore_signal(barrier, inc=1, device_id=other, device_id_type=MESH)
    fetches = [
        pltpu.make_async_copy(src, dst, sems.at[i])
        for i, (src, dst) in enumerate(zip(refs[:4], scratch[:4]))
    ]
    for fetch in fetches:
        fetch.start()
    if partnered:
        pl.semaphore_wait(barrier, 2)
        half = refs[0].shape[0] // 2
        mine = pl.ds(part * half, half)
        copy, forward = [
            pltpu.make_async_remote_copy(
                src_ref=src.at[mine],
                dst_ref=outs[4].at[mine],
                send_sem=send_sem.at[i],
                recv_sem=recv_sem.at[i],
                device_id=other,
                device_id_type=MESH,
            )
            for i, (src, other) in enumerate(((refs[0], partner), (outs[4], twin)))
        ]
        copy.start()
    for fetch in fetches:
        fetch.wait()

    stores = [
        pltpu.make_async_copy(src, dst, sems.at[4 + i])
        for i, (src, dst) in enumerate(zip(built, outs[:4]))
    ]
    for i, axis in enumerate(("col", "row")):
        side_ref = built[i]
        width = side_ref.shape[1]
        for j in range(width // TILE):
            cols = pl.ds(j * TILE, TILE)
            signed = signed_atoms(pairs_ref, lax.axis_index(axis) * width + j * TILE)
            side_ref[:ATOMS, cols] = signed
            side_ref[ATOMS:, cols] = features(blocks_ref, signed)
        stores[i].start()
        if partnered and i == 0:
            copy.wait_recv()
            forward.start()

    lag = lag_ref[0]
    counts = weigh(draw_ref, slot_ref)
    t_row = lax.broadcasted_iota(jnp.int32, (BLOCK_LEN, frames), 0)
    lane = lax.broadcasted_iota(jnp.int32, (BLOCK_LEN, frames), 1)
    t_lane = lane % BLOCK_LEN
    uses = jnp.where(t_lane < BLOCK_LEN - lag, 1.0, 0.0) + jnp.where(t_lane >= lag, 1.0, 0.0)
    same = jnp.where(t_lane == t_row, uses, 0.0)
    apart = jnp.where(jnp.abs(t_lane - t_row) == lag, 1.0, 0.0)
    mean_w = jnp.zeros((BLOCK_LEN, frames), jnp.float32)
    for b, n in enumerate(counts):
        share = jnp.where(lane // BLOCK_LEN == b, n, 0.0)
        mean_w = mean_w + share * uses
        weigh_ref[pl.ds(b * BLOCK_LEN, BLOCK_LEN), :] = (share * same).astype(jnp.bfloat16)
        weigh_ref[pl.ds(frames + b * BLOCK_LEN, BLOCK_LEN), :] = (share * apart).astype(
            jnp.bfloat16
        )
    weigh_ref[pl.ds(2 * frames, 16), :] = mean_w[:16].astype(jnp.bfloat16)
    inv_ref[...] = 1.0 / jnp.full((8, 128), (2 * DRAWS * (BLOCK_LEN - lag)).astype(jnp.float32))
    for store in stores[2:]:
        store.start()
    for store in stores:
        store.wait()
    if partnered:
        copy.wait_send()
        forward.wait()


def near_side(blocks, partnered, weigh, lag_time, resample, block_slot, atom_pairs):
    held = blocks.shape[0] * BLOCK_LEN
    frames = held * (2 if partnered else 1)
    built = [
        ((ATOMS + held, F // lax.axis_size("col")), jnp.bfloat16),
        ((ATOMS + held, F // lax.axis_size("row")), jnp.bfloat16),
        ((2 * frames + 16, frames), jnp.bfloat16),
        ((8, 128), jnp.float32),
    ]
    outs = [jax.ShapeDtypeStruct(*shape) for shape in built]
    if partnered:
        outs.append(jax.ShapeDtypeStruct(blocks.shape, blocks.dtype))
    return pl.pallas_call(
        functools.partial(near_kernel, partnered, weigh),
        out_shape=outs,
        in_specs=[pl.BlockSpec(memory_space=pltpu.HBM)] * 4
        + [pl.BlockSpec(memory_space=pltpu.SMEM)],
        out_specs=[pl.BlockSpec(memory_space=pltpu.HBM)] * len(outs),
        scratch_shapes=[
            pltpu.VMEM(blocks.shape, blocks.dtype),
            pltpu.SMEM(resample.shape, jnp.int32),
            pltpu.SMEM(block_slot.shape, jnp.int32),
            pltpu.VMEM(atom_pairs.shape, jnp.int32),
            *[pltpu.VMEM(*shape) for shape in built],
            pltpu.SemaphoreType.DMA((8,)),
            pltpu.SemaphoreType.DMA((2,)),
            pltpu.SemaphoreType.DMA((2,)),
        ],
        compiler_params=pltpu.CompilerParams(
            vmem_limit_bytes=VMEM_BYTES,
            **(dict(collective_id=0, has_side_effects=True) if partnered else {}),
        ),
        name="near_side",
    )(blocks, resample, block_slot, atom_pairs, lag_time)


def cov_kernel(inputs, *refs):
    inst_ref, lagged_ref = refs[inputs : inputs + 2]
    held_refs = refs[inputs + 2 : -4]
    c_ref, turned_ref, ds_ref, sems = refs[-4:]
    col_ref, row_ref, weigh_ref, inv_ref, *far_refs = held_refs
    frames = weigh_ref.shape[1]
    inv = lambda: inv_ref[0:1, 0:1]

    @pl.when(pl.program_id(0) == 0)
    def _():
        fetches = [
            pltpu.make_async_copy(
                src, dst.at[pl.ds(0, src.shape[0])] if i < 2 else dst, sems.at[i]
            )
            for i, (src, dst) in enumerate(zip(refs[:inputs], held_refs))
        ]
        for fetch in fetches[4:] + fetches[:4]:
            fetch.start()
        for fetch in fetches[4:]:
            fetch.wait()
        for fetch, side_ref in zip(fetches, (col_ref, row_ref)):
            fetch.wait()
            for j in range(side_ref.shape[1] // TILE):
                cols = pl.ds(j * TILE, TILE)
                at = ATOMS + frames - len(far_refs) * (frames // 2)
                for far_ref in far_refs:
                    side_ref[at:, cols] = features(far_ref, side_ref[:ATOMS, cols])
        for fetch in fetches[2:4]:
            fetch.wait()
        mean_w = weigh_ref[pl.ds(2 * frames, 16), :]
        means = [
            dot(mean_w, side_ref[ATOMS:, :])[0:1] * inv() for side_ref in (col_ref, row_ref)
        ]
        for j in range(ds_ref.shape[0]):
            cols = pl.ds(j * TILE, TILE)
            f = col_ref[ATOMS:, cols].astype(jnp.float32)
            c_ref[:, cols] = (f - means[0][:, j * TILE : (j + 1) * TILE]).astype(jnp.bfloat16)
        for j in range(turned_ref.shape[0] // TILE):
            cols = pl.ds(j * TILE, TILE)
            f = row_ref[ATOMS:, cols].astype(jnp.float32)
            c = (f - means[1][:, j * TILE : (j + 1) * TILE]).astype(jnp.bfloat16)
            turned_ref[cols, :] = c.T
        for j in range(ds_ref.shape[0]):
            ds_ref[j] = (
                dot(weigh_ref[pl.ds(0, 2 * frames), :], c_ref[:, pl.ds(j * TILE, TILE)]) * inv()
            ).astype(jnp.bfloat16)

    j = pl.program_id(0)
    c = turned_ref[...]
    inst_ref[0] = dot(c, ds_ref[j, pl.ds(0, frames), :]).astype(jnp.bfloat16)
    lagged_ref[0] = dot(c, ds_ref[j, pl.ds(frames, frames), :]).astype(jnp.bfloat16)


def covariances(sides):
    frames = sides[2].shape[1]
    height = F // lax.axis_size("row")
    width = F // lax.axis_size("col")
    out = jax.ShapeDtypeStruct((1, height, width), jnp.bfloat16)
    out_spec = pl.BlockSpec((1, height, TILE), lambda j: (0, 0, j))
    return pl.pallas_call(
        functools.partial(cov_kernel, len(sides)),
        grid=(width // TILE,),
        out_shape=(out, out),
        in_specs=[pl.BlockSpec(memory_space=pltpu.HBM)] * len(sides),
        out_specs=(out_spec, out_spec),
        scratch_shapes=[
            pltpu.VMEM((ATOMS + frames, width), jnp.bfloat16),
            pltpu.VMEM((ATOMS + frames, height), jnp.bfloat16),
            *[pltpu.VMEM(side.shape, side.dtype) for side in sides[2:]],
            pltpu.VMEM((frames, width), jnp.bfloat16),
            pltpu.VMEM((height, frames), jnp.bfloat16),
            pltpu.VMEM((width // TILE, 2 * frames, TILE), jnp.bfloat16),
            pltpu.SemaphoreType.DMA((len(sides),)),
        ],
        compiler_params=pltpu.CompilerParams(vmem_limit_bytes=VMEM_BYTES),
        name="covariances",
    )(*sides)


def shards(coordinates, resample, block_slot, lag_time, atom_pairs):
    blk_count = coordinates.shape[0]
    halves = blk_count % 2 == 0 and lax.axis_size("col") % 2 == 0
    partnered = lax.axis_size("rep") == 2 and 2 * blk_count <= DRAWS and halves
    if partnered:
        blocks = coordinates

        def weigh(draw_ref, slot_ref):
            mine = lax.axis_index("rep") * blk_count
            slots = [slot_ref[draw_ref[0, d]] for d in range(DRAWS)]
            return [
                sum(jnp.where(s == first + b, 1.0, 0.0) for s in slots)
                for first in (mine, blk_count - mine)
                for b in range(blk_count)
            ]
    else:
        spare = -DRAWS % (128 // BLOCK_LEN)
        blocks = drawn_blocks(coordinates, resample, block_slot)
        blocks = jnp.pad(blocks, ((0, spare), (0, 0), (0, 0), (0, 0)))

        def weigh(draw_ref, slot_ref):
            return [1.0] * DRAWS + [0.0] * spare
    sides = near_side(
        blocks.transpose(0, 2, 1, 3), partnered, weigh, lag_time, resample, block_slot, atom_pairs
    )
    return covariances(sides)


def solution(mesh):
    return jax.shard_map(
        shards,
        mesh=mesh,
        in_specs=(P("rep", None, None, None), P("rep", None), P(), P("rep"), P()),
        out_specs=(P("rep", "row", "col"), P("rep", "row", "col")),
        check_vma=False,
    )
```

```python
import functools

import jax
import jax.numpy as jnp
from jax import lax
from jax.experimental import pallas as pl
from jax.experimental.pallas import tpu as pltpu
from jax.sharding import PartitionSpec as P

F = 4096
ATOMS = 128
BLOCK_LEN = 32
DRAWS = 22
TILE = 256
TINY = 1.2e-38
VMEM_BYTES = 60 * 1024 * 1024
MESH = pl.DeviceIdType.MESH


def slot_lookup(lists, slot_table):
    matches = lists[..., None] == jnp.arange(slot_table.shape[0], dtype=jnp.int32)
    return jnp.sum(jnp.where(matches, slot_table, 0), axis=-1)


def owner_rank(lists, slot_table, blk_count):
    slots = slot_lookup(lists, slot_table)
    owner_ids = slots // blk_count
    local_ids = slots % blk_count
    draw_ids = jnp.arange(lists.shape[-1], dtype=jnp.int32)
    before = (owner_ids[..., :, None] == owner_ids[..., None, :]) & (
        draw_ids[None, :] < draw_ids[:, None]
    )
    ranks = jnp.sum(before.astype(jnp.int32), axis=-1)
    return (owner_ids, local_ids, ranks)


def pack_requests(resample, block_slot, local_data, capacity):
    every_list = lax.all_gather(resample, "rep", axis=0, tiled=True)
    blk_count = local_data.shape[0]
    owners_all, local_all, ranks_all = owner_rank(every_list, block_slot, blk_count)
    myself = lax.axis_index("rep")
    wanted = (owners_all == myself)[:, :, None] & (
        ranks_all[:, :, None] == jnp.arange(capacity, dtype=jnp.int32)
    )
    picked = local_all[:, :, None] == jnp.arange(blk_count, dtype=jnp.int32)
    selector = jnp.einsum(
        "rdc,rdk->rck", wanted.astype(jnp.float32), picked.astype(jnp.float32)
    ).astype(jnp.bfloat16)
    return jnp.einsum(
        "rck,kx->rcx", selector, local_data, preferred_element_type=jnp.float32
    ).astype(jnp.bfloat16)


def unpack_blocks(received, resample, block_slot, blk_count, capacity):
    owner_ids, local_ids, ranks = owner_rank(resample[0], block_slot, blk_count)
    rows_wanted = owner_ids * capacity + ranks
    flat = received.reshape(-1, received.shape[-1])
    return jnp.take(flat, rows_wanted, axis=0)


def drawn_blocks(coordinates, resample, block_slot):
    rep_total = lax.axis_size("rep")
    per_owner = (DRAWS + rep_total - 1) // rep_total
    capacity = max(2, per_owner + per_owner // 2)
    blk_count = coordinates.shape[0]
    outgoing = pack_requests(resample, block_slot, coordinates.reshape(blk_count, -1), capacity)
    received = lax.all_to_all(outgoing, "rep", split_axis=0, concat_axis=0, tiled=True)
    return unpack_blocks(received, resample, block_slot, blk_count, capacity).reshape(
        DRAWS, BLOCK_LEN, 3, ATOMS
    )


def dot(a, b):
    return jnp.dot(a, b, preferred_element_type=jnp.float32)


def signed_atoms(pairs_ref, first):
    ids = lax.broadcasted_iota(jnp.int32, (ATOMS, TILE), 0)
    cols = pl.ds(pl.multiple_of(first, TILE), TILE)
    a = pairs_ref[0:1, cols]
    b = pairs_ref[1:2, cols]
    return jnp.where(ids == a, 1.0, jnp.where(ids == b, -1.0, 0.0)).astype(jnp.bfloat16)


def features(blocks_ref, signed):
    squared = 0.0
    for k in range(3):
        difference = dot(blocks_ref[:, k].reshape(-1, ATOMS), signed)
        squared = squared + difference * difference
    return (squared * lax.rsqrt(jnp.maximum(squared, TINY))).astype(jnp.bfloat16)


def near_kernel(partnered, weigh, *refs):
    outs, scratch = refs[5:-11], refs[-11:]
    lag_ref = refs[4]
    blocks_ref, draw_ref, slot_ref, pairs_ref = scratch[:4]
    built = col_ref, row_ref, weigh_ref, inv_ref = scratch[4:8]
    sems, send_sem, recv_sem = scratch[8:]
    frames = weigh_ref.shape[1]

    if partnered:
        partner = {"rep": 1 - lax.axis_index("rep")}
        barrier = pltpu.get_barrier_semaphore()
        pl.semaphore_signal(barrier, inc=1, device_id=partner, device_id_type=MESH)
    fetches = [
        pltpu.make_async_copy(src, dst, sems.at[i])
        for i, (src, dst) in enumerate(zip(refs[:4], scratch[:4]))
    ]
    for fetch in fetches:
        fetch.start()
    if partnered:
        pl.semaphore_wait(barrier, 1)
        copy = pltpu.make_async_remote_copy(
            src_ref=refs[0],
            dst_ref=outs[4],
            send_sem=send_sem,
            recv_sem=recv_sem,
            device_id=partner,
            device_id_type=MESH,
        )
        copy.start()
    for fetch in fetches:
        fetch.wait()

    stores = [
        pltpu.make_async_copy(src, dst, sems.at[4 + i])
        for i, (src, dst) in enumerate(zip(built, outs[:4]))
    ]
    for i, axis in enumerate(("col", "row")):
        side_ref = built[i]
        width = side_ref.shape[1]
        for j in range(width // TILE):
            cols = pl.ds(j * TILE, TILE)
            signed = signed_atoms(pairs_ref, lax.axis_index(axis) * width + j * TILE)
            side_ref[:ATOMS, cols] = signed
            side_ref[ATOMS:, cols] = features(blocks_ref, signed)
        stores[i].start()

    lag = lag_ref[0]
    counts = weigh(draw_ref, slot_ref)
    t_row = lax.broadcasted_iota(jnp.int32, (BLOCK_LEN, frames), 0)
    lane = lax.broadcasted_iota(jnp.int32, (BLOCK_LEN, frames), 1)
    t_lane = lane % BLOCK_LEN
    uses = jnp.where(t_lane < BLOCK_LEN - lag, 1.0, 0.0) + jnp.where(t_lane >= lag, 1.0, 0.0)
    same = jnp.where(t_lane == t_row, uses, 0.0)
    apart = jnp.where(jnp.abs(t_lane - t_row) == lag, 1.0, 0.0)
    mean_w = jnp.zeros((BLOCK_LEN, frames), jnp.float32)
    for b, n in enumerate(counts):
        share = jnp.where(lane // BLOCK_LEN == b, n, 0.0)
        mean_w = mean_w + share * uses
        weigh_ref[pl.ds(b * BLOCK_LEN, BLOCK_LEN), :] = (share * same).astype(jnp.bfloat16)
        weigh_ref[pl.ds(frames + b * BLOCK_LEN, BLOCK_LEN), :] = (share * apart).astype(
            jnp.bfloat16
        )
    weigh_ref[pl.ds(2 * frames, 16), :] = mean_w[:16].astype(jnp.bfloat16)
    inv_ref[...] = 1.0 / jnp.full((8, 128), (2 * DRAWS * (BLOCK_LEN - lag)).astype(jnp.float32))
    for store in stores[2:]:
        store.start()
    for store in stores:
        store.wait()
    if partnered:
        copy.wait()


def near_side(blocks, partnered, weigh, lag_time, resample, block_slot, atom_pairs):
    held = blocks.shape[0] * BLOCK_LEN
    frames = held * (2 if partnered else 1)
    built = [
        ((ATOMS + held, F // lax.axis_size("col")), jnp.bfloat16),
        ((ATOMS + held, F // lax.axis_size("row")), jnp.bfloat16),
        ((2 * frames + 16, frames), jnp.bfloat16),
        ((8, 128), jnp.float32),
    ]
    outs = [jax.ShapeDtypeStruct(*shape) for shape in built]
    if partnered:
        outs.append(jax.ShapeDtypeStruct(blocks.shape, blocks.dtype))
    return pl.pallas_call(
        functools.partial(near_kernel, partnered, weigh),
        out_shape=outs,
        in_specs=[pl.BlockSpec(memory_space=pltpu.HBM)] * 4
        + [pl.BlockSpec(memory_space=pltpu.SMEM)],
        out_specs=[pl.BlockSpec(memory_space=pltpu.HBM)] * len(outs),
        scratch_shapes=[
            pltpu.VMEM(blocks.shape, blocks.dtype),
            pltpu.SMEM(resample.shape, jnp.int32),
            pltpu.SMEM(block_slot.shape, jnp.int32),
            pltpu.VMEM(atom_pairs.shape, jnp.int32),
            *[pltpu.VMEM(*shape) for shape in built],
            pltpu.SemaphoreType.DMA((8,)),
            pltpu.SemaphoreType.DMA,
            pltpu.SemaphoreType.DMA,
        ],
        compiler_params=pltpu.CompilerParams(
            vmem_limit_bytes=VMEM_BYTES,
            **(dict(collective_id=0, has_side_effects=True) if partnered else {}),
        ),
        name="near_side",
    )(blocks, resample, block_slot, atom_pairs, lag_time)


def cov_kernel(inputs, *refs):
    inst_ref, lagged_ref = refs[inputs : inputs + 2]
    held_refs = refs[inputs + 2 : -4]
    c_ref, turned_ref, ds_ref, sems = refs[-4:]
    col_ref, row_ref, weigh_ref, inv_ref, *far_refs = held_refs
    frames = weigh_ref.shape[1]
    inv = lambda: inv_ref[0:1, 0:1]

    @pl.when(pl.program_id(0) == 0)
    def _():
        fetches = [
            pltpu.make_async_copy(
                src, dst.at[pl.ds(0, src.shape[0])] if i < 2 else dst, sems.at[i]
            )
            for i, (src, dst) in enumerate(zip(refs[:inputs], held_refs))
        ]
        for fetch in fetches:
            fetch.start()
        for fetch in fetches:
            fetch.wait()
        for side_ref in (col_ref, row_ref):
            for j in range(side_ref.shape[1] // TILE):
                cols = pl.ds(j * TILE, TILE)
                at = ATOMS + frames - len(far_refs) * (frames // 2)
                for far_ref in far_refs:
                    side_ref[at:, cols] = features(far_ref, side_ref[:ATOMS, cols])
        mean_w = weigh_ref[pl.ds(2 * frames, 16), :]
        means = [
            dot(mean_w, side_ref[ATOMS:, :])[0:1] * inv() for side_ref in (col_ref, row_ref)
        ]
        for j in range(ds_ref.shape[0]):
            cols = pl.ds(j * TILE, TILE)
            f = col_ref[ATOMS:, cols].astype(jnp.float32)
            c_ref[:, cols] = (f - means[0][:, j * TILE : (j + 1) * TILE]).astype(jnp.bfloat16)
        for j in range(turned_ref.shape[0] // TILE):
            cols = pl.ds(j * TILE, TILE)
            f = row_ref[ATOMS:, cols].astype(jnp.float32)
            c = (f - means[1][:, j * TILE : (j + 1) * TILE]).astype(jnp.bfloat16)
            turned_ref[cols, :] = c.T
        for j in range(ds_ref.shape[0]):
            ds_ref[j] = (
                dot(weigh_ref[pl.ds(0, 2 * frames), :], c_ref[:, pl.ds(j * TILE, TILE)]) * inv()
            ).astype(jnp.bfloat16)

    tiles = inst_ref.shape[2] // TILE
    c = turned_ref[...]
    for i in range(tiles):
        j = pl.program_id(0) * tiles + i
        cols = pl.ds(i * TILE, TILE)
        inst_ref[0, :, cols] = dot(c, ds_ref[j, pl.ds(0, frames), :]).astype(jnp.bfloat16)
        lagged_ref[0, :, cols] = dot(c, ds_ref[j, pl.ds(frames, frames), :]).astype(jnp.bfloat16)


def covariances(sides):
    frames = sides[2].shape[1]
    height = F // lax.axis_size("row")
    width = F // lax.axis_size("col")
    out = jax.ShapeDtypeStruct((1, height, width), jnp.bfloat16)
    out_spec = pl.BlockSpec((1, height, 2 * TILE), lambda j: (0, 0, j))
    return pl.pallas_call(
        functools.partial(cov_kernel, len(sides)),
        grid=(width // (2 * TILE),),
        out_shape=(out, out),
        in_specs=[pl.BlockSpec(memory_space=pltpu.HBM)] * len(sides),
        out_specs=(out_spec, out_spec),
        scratch_shapes=[
            pltpu.VMEM((ATOMS + frames, width), jnp.bfloat16),
            pltpu.VMEM((ATOMS + frames, height), jnp.bfloat16),
            *[pltpu.VMEM(side.shape, side.dtype) for side in sides[2:]],
            pltpu.VMEM((frames, width), jnp.bfloat16),
            pltpu.VMEM((height, frames), jnp.bfloat16),
            pltpu.VMEM((width // TILE, 2 * frames, TILE), jnp.bfloat16),
            pltpu.SemaphoreType.DMA((len(sides),)),
        ],
        compiler_params=pltpu.CompilerParams(vmem_limit_bytes=VMEM_BYTES),
        name="covariances",
    )(*sides)


def shards(coordinates, resample, block_slot, lag_time, atom_pairs):
    blk_count = coordinates.shape[0]
    partnered = lax.axis_size("rep") == 2 and 2 * blk_count <= DRAWS
    if partnered:
        blocks = coordinates

        def weigh(draw_ref, slot_ref):
            mine = lax.axis_index("rep") * blk_count
            slots = [slot_ref[draw_ref[0, d]] for d in range(DRAWS)]
            return [
                sum(jnp.where(s == first + b, 1.0, 0.0) for s in slots)
                for first in (mine, blk_count - mine)
                for b in range(blk_count)
            ]
    else:
        spare = -DRAWS % (128 // BLOCK_LEN)
        blocks = drawn_blocks(coordinates, resample, block_slot)
        blocks = jnp.pad(blocks, ((0, spare), (0, 0), (0, 0), (0, 0)))

        def weigh(draw_ref, slot_ref):
            return [1.0] * DRAWS + [0.0] * spare
    sides = near_side(
        blocks.transpose(0, 2, 1, 3), partnered, weigh, lag_time, resample, block_slot, atom_pairs
    )
    return covariances(sides)


def solution(mesh):
    return jax.shard_map(
        shards,
        mesh=mesh,
        in_specs=(P("rep", None, None, None), P("rep", None), P(), P("rep"), P()),
        out_specs=(P("rep", "row", "col"), P("rep", "row", "col")),
        check_vma=False,
    )
```
